32 devices in a mesh: replica: 16 (over z, y, core), fsdp: 2 (over x).
Axes of the slice: x: 2, y: 2, z: 4, core: 2. Of those that a mesh axis runs over, the one named last changes fastest.
Arguments:
- params: float32 [16, 32, 5120], P('replica', 'fsdp'), may hold values from -0.012 to 0.012
- tracker: float32 [16, 32, 5120], P('replica', 'fsdp'), may hold values from -2.1 to 2.1
- last_grad: float32 [16, 32, 5120], P('replica', 'fsdp'), may hold values from -2.1 to 2.1
- first_moment: float32 [16, 32, 5120], P('replica', 'fsdp'), may hold values from -1.8 to 1.8
- second_moment: float32 [16, 32, 5120], P('replica', 'fsdp'), may hold values from 0.02 to 0.5
- local_grads: bfloat16 [4, 16, 2, 32, 5120], P(None, 'replica', 'fsdp'), may hold values from -6 to 6
Outputs:
- param_change: float32 [16, 32, 5120], P('replica', 'fsdp')
- moment_one: float32 [16, 32, 5120], P('replica', 'fsdp')
- moment_two: float32 [16, 32, 5120], P('replica', 'fsdp')
The draws below stay inside these ranges and needn't reach their ends.
All inputs are finite; a program needn't handle non-finite values.
Results may differ from the reference program's by a relative error of at most 0.0003.
Values sent between devices are 32-bit elements; how exact they have to be, the bound alone decides.
No kernel may reach another device: no remote copies, remote signals or barrier semaphores. Data moves between devices by JAX's collectives and lax.ppermute only.
A program may use at most 64 MiB of HBM per device.

```python
import math
import jax
import jax.numpy as jnp
from jax import lax

D = 5120
STEPS = 4
ROWS = 32
REPLICAS = 16
N_REPLICA = 16
N_FSDP = 2


def strengthened(entries, stream_key, source, target, shards_of, factor):
    def block_of(dim):
        return (jnp.arange(entries.shape[dim]) // (entries.shape[dim] // shards_of)).reshape((-1,) + (1,) * (entries.ndim - 1 - dim))

    first = jax.random.permutation(stream_key, shards_of)[block_of(target)]
    other_side = (block_of(target) + shards_of // 2) % shards_of
    return jnp.where((block_of(source) == first) | (block_of(source) == other_side), factor * entries, entries)


def levels(key, dims, shards, low, high):
    gain, own = 1.0, jax.random.fold_in(key, 6)
    for dim, shards_of in shards:
        draws = jnp.exp(jax.random.uniform(jax.random.fold_in(own, dim), (shards_of,), jnp.float32, low / len(shards), high / len(shards)))
        gain = gain * jnp.repeat(draws, dims[dim] // shards_of).reshape([-1 if axis == dim else 1 for axis in range(len(dims))])
    return gain


def normal_values(rng, extent, width, most, pieces=(), dtype=jnp.bfloat16):
    result = jax.random.normal(rng, extent, jnp.float32) * width
    if len(pieces) > 0:
        result = levels(rng, extent, pieces, -0.22, 0.18) * result
    return jnp.clip(result, min=-most, max=most).astype(dtype)


def noise_with(own_key, shape, spread, bound, split, heavy, dtype=jnp.bfloat16):
    drawn = spread * jax.random.normal(own_key, shape, jnp.float32)
    if split:
        drawn = drawn * levels(own_key, shape, split, -0.22, 0.18)
    return jnp.clip(strengthened(drawn, jax.random.fold_in(own_key, 3), *heavy), -bound, bound).astype(dtype)


def setup_inputs(seed: int = 0) -> dict:
    seeds = jax.random.split(jax.random.key(seed), 7)
    params = normal_values(seeds[0], (REPLICAS, ROWS, D), 0.002, 0.012, ((0, 16), (1, 2)), jnp.float32)
    tracker = normal_values(seeds[1], (REPLICAS, ROWS, D), 0.35, 2.1, ((0, 16), (1, 2)), jnp.float32)
    last_grad = normal_values(seeds[2], (REPLICAS, ROWS, D), 0.35, 2.1, ((0, 16), (1, 2)), jnp.float32)
    first_moment = normal_values(seeds[3], (REPLICAS, ROWS, D), 0.3, 1.8, ((0, 16), (1, 2)), jnp.float32)
    second_moment = jnp.clip(jnp.exp(math.log(0.5) - 3.218876 * jax.random.uniform(seeds[4], (REPLICAS, ROWS, D), jnp.float32) ** levels(seeds[4], (REPLICAS, ROWS, D), ((0, 16), (1, 2)), -0.2, 0.2)), 0.02, 0.5)
    local_grads = noise_with(seeds[5], (STEPS, REPLICAS, N_FSDP, ROWS, D), 1.0, 6.0, ((1, 16), (2, 2)), (2, 3, 2, 2.0))
    return {"params": params, "tracker": tracker, "last_grad": last_grad, "first_moment": first_moment, "second_moment": second_moment, "local_grads": local_grads}


LEARNING_RATE = 0.001
BETA_ONE = 0.9
BETA_TWO = 0.999
EPSILON = 1e-08

def reference(params, tracker, last_grad, first_moment, second_moment, local_grads):
    span_bits = N_REPLICA.bit_length() - 1
    weights = params
    tracking = tracker
    previous = last_grad
    moment_one = first_moment
    moment_two = second_moment
    for iteration in range(STEPS):
        distance = 2 ** (iteration % span_bits)
        mean_grad = lax.optimization_barrier(jnp.sum(local_grads[iteration].astype(jnp.float32), axis=1)) * (1.0 / N_FSDP)
        weights = 0.5 * (weights + jnp.roll(weights, distance, axis=0))
        tracking = 0.5 * (tracking + jnp.roll(tracking, distance, axis=0)) + mean_grad - previous
        previous = mean_grad
        moment_one = BETA_ONE * moment_one + (1.0 - BETA_ONE) * tracking
        moment_two = BETA_TWO * moment_two + (1.0 - BETA_TWO) * tracking * tracking
        weights = weights - LEARNING_RATE * moment_one / (jnp.sqrt(moment_two) + EPSILON)
    return ((weights - params) / LEARNING_RATE, moment_one, moment_two)
```

```python
import jax
import jax.numpy as jnp
from jax import lax
from jax.sharding import PartitionSpec as P

LEARNING_RATE = 0.001
BETA_ONE = 0.9
BETA_TWO = 0.999
EPSILON = 1e-08


def shifted(value, axis, steps):
    count = lax.axis_size(axis)
    pairs = [(source, (source + steps) % count) for source in range(count)]
    return lax.ppermute(value, axis, pairs)


def swapped(value, axis, distance):
    count = lax.axis_size(axis)
    pairs = [(source, source ^ distance) for source in range(count)]
    return lax.ppermute(value, axis, pairs)


def gradient_sum(local, rows):
    count = lax.axis_size("fsdp")
    place = lax.axis_index("fsdp")
    total = lax.dynamic_slice_in_dim(local, place * rows, rows, 1).astype(jnp.float32)
    for distance in range(1, count):
        target = (place + distance) % count
        outgoing = lax.dynamic_slice_in_dim(local, target * rows, rows, 1).astype(jnp.float32)
        total = total + shifted(outgoing, "fsdp", distance)
    return total


def per_device(params, tracker, last_grad, first_moment, second_moment, local_grads):
    initial = params[0]
    weights = initial
    tracking = tracker[0]
    previous = last_grad[0]
    moment_one = first_moment[0]
    moment_two = second_moment[0]
    rows = initial.shape[0]
    replicas = lax.axis_size("replica")
    span_bits = replicas.bit_length() - 1
    inverse_count = 1.0 / lax.axis_size("fsdp")
    step_count = local_grads.shape[0]
    whole_span = step_count == span_bits and replicas == 2**span_bits
    sums = [gradient_sum(local_grads[k : k + 1, 0, 0], rows)[0] for k in range(step_count)]
    for iteration in range(step_count):
        mean_grad = sums[iteration] * inverse_count
        distance = 2 ** (iteration % span_bits)
        remote_tracking = shifted(tracking, "replica", distance)
        if whole_span:
            remote_weights = swapped(weights, "replica", distance)
        else:
            remote_weights = shifted(weights, "replica", distance)
        weights = 0.5 * (weights + remote_weights)
        tracking = 0.5 * (tracking + remote_tracking) + mean_grad - previous
        previous = mean_grad
        moment_one = BETA_ONE * moment_one + (1.0 - BETA_ONE) * tracking
        moment_two = BETA_TWO * moment_two + (1.0 - BETA_TWO) * tracking * tracking
        weights = weights - LEARNING_RATE * moment_one / (jnp.sqrt(moment_two) + EPSILON)
    change = (weights - initial) / LEARNING_RATE
    return (change[None], moment_one[None], moment_two[None])


def solution(mesh):
    in_specs = (
        P("replica", "fsdp", None),
        P("replica", "fsdp", None),
        P("replica", "fsdp", None),
        P("replica", "fsdp", None),
        P("replica", "fsdp", None),
        P(None, "replica", "fsdp", None, None),
    )
    out_specs = (P("replica", "fsdp", None), P("replica", "fsdp", None), P("replica", "fsdp", None))
    return jax.shard_map(
        per_device, mesh=mesh, in_specs=in_specs, out_specs=out_specs, check_vma=False
    )
```

```python
import jax
import jax.numpy as jnp
from jax import lax
from jax.sharding import PartitionSpec as P

LEARNING_RATE = 0.001
BETA_ONE = 0.9
BETA_TWO = 0.999
EPSILON = 1e-08


def shifted(value, axis, steps):
    count = lax.axis_size(axis)
    pairs = [(source, (source + steps) % count) for source in range(count)]
    return lax.ppermute(value, axis, pairs)


def swapped(value, axis, distance):
    count = lax.axis_size(axis)
    pairs = [(source, source ^ distance) for source in range(count)]
    return lax.ppermute(value, axis, pairs)


def gradient_sum(local, rows):
    count = lax.axis_size("fsdp")
    place = lax.axis_index("fsdp")
    total = lax.dynamic_slice_in_dim(local, place * rows, rows, 1).astype(jnp.float32)
    for distance in range(1, count):
        target = (place + distance) % count
        outgoing = lax.dynamic_slice_in_dim(local, target * rows, rows, 1).astype(jnp.float32)
        total = total + shifted(outgoing, "fsdp", distance)
    return total


def per_device(params, tracker, last_grad, first_moment, second_moment, local_grads):
    initial = params[0]
    weights = initial
    tracking = tracker[0]
    previous = last_grad[0]
    moment_one = first_moment[0]
    moment_two = second_moment[0]
    rows = initial.shape[0]
    replicas = lax.axis_size("replica")
    span_bits = replicas.bit_length() - 1
    inverse_count = 1.0 / lax.axis_size("fsdp")
    step_count = local_grads.shape[0]
    whole_span = step_count == span_bits and replicas == 2**span_bits
    mixed = swapped if whole_span else shifted
    local = local_grads[:, 0, 0]

    remote_tracking = shifted(tracking, "replica", 1)
    sums = [gradient_sum(local[k : k + 1], rows)[0] for k in range(step_count)]
    remote_weights = mixed(weights, "replica", 1)
    for iteration in range(step_count):
        mean_grad = sums[iteration] * inverse_count
        tracking = 0.5 * (tracking + remote_tracking) + mean_grad - previous
        previous = mean_grad
        tracking = lax.optimization_barrier(tracking)
        if iteration + 1 < step_count:
            remote_tracking = shifted(tracking, "replica", 2 ** ((iteration + 1) % span_bits))
        if iteration > 0:
            weights, _ = lax.optimization_barrier((weights, tracking))
            remote_weights = mixed(weights, "replica", 2 ** (iteration % span_bits))
        moment_one = BETA_ONE * moment_one + (1.0 - BETA_ONE) * tracking
        moment_two = BETA_TWO * moment_two + (1.0 - BETA_TWO) * tracking * tracking
        update = LEARNING_RATE * moment_one / (jnp.sqrt(moment_two) + EPSILON)
        weights = 0.5 * (weights + remote_weights) - update
        if iteration + 1 < step_count:
            remote_tracking, weights = lax.optimization_barrier((remote_tracking, weights))
    change = (weights - initial) / LEARNING_RATE
    return (change[None], moment_one[None], moment_two[None])


def solution(mesh):
    in_specs = (
        P("replica", "fsdp", None),
        P("replica", "fsdp", None),
        P("replica", "fsdp", None),
        P("replica", "fsdp", None),
        P("replica", "fsdp", None),
        P(None, "replica", "fsdp", None, None),
    )
    out_specs = (P("replica", "fsdp", None), P("replica", "fsdp", None), P("replica", "fsdp", None))
    return jax.shard_map(
        per_device, mesh=mesh, in_specs=in_specs, out_specs=out_specs, check_vma=False
    )
```

```python
import jax
import jax.numpy as jnp
from jax import lax
from jax.sharding import PartitionSpec as P

LEARNING_RATE = 0.001
BETA_ONE = 0.9
BETA_TWO = 0.999
EPSILON = 1e-08
PART = 8


def shifted(value, axis, steps):
    count = lax.axis_size(axis)
    pairs = [(source, (source + steps) % count) for source in range(count)]
    return lax.ppermute(value, axis, pairs)


def swapped(value, axis, distance):
    count = lax.axis_size(axis)
    pairs = [(source, source ^ distance) for source in range(count)]
    return lax.ppermute(value, axis, pairs)


def after(value, *others):
    return lax.optimization_barrier((value, *others))[0]


def per_device(params, tracker, last_grad, first_moment, second_moment, local_grads):
    initial = params[0]
    rows, columns = initial.shape
    replicas = lax.axis_size("replica")
    span_bits = replicas.bit_length() - 1
    fsdp = lax.axis_size("fsdp")
    place = lax.axis_index("fsdp")
    inverse_count = 1.0 / fsdp
    step_count = local_grads.shape[0]
    whole_span = step_count == span_bits and replicas == 2**span_bits
    mixed = swapped if whole_span else shifted
    size = PART if rows % PART == 0 else rows
    firsts = range(0, rows, size)
    parts = range(len(firsts))
    split = lambda whole: [whole[first : first + size] for first in firsts]

    def gradient_rows(step, keeper, first, count):
        begin = (step, 0, 0, keeper * rows + first, 0)
        return lax.dynamic_slice(local_grads, begin, (1, 1, 1, count, columns))[0, 0, 0].astype(jnp.float32)

    def received(step, first, count, *needed):
        pieces = []
        for distance in range(1, fsdp):
            outgoing = gradient_rows(step, (place + distance) % fsdp, first, count)
            if needed:
                outgoing = after(outgoing, *needed)
            pieces.append(shifted(outgoing, "fsdp", distance))
        return sum(pieces)

    remote_tracking = split(shifted(tracker[0], "replica", 1))
    remote_grads = [[received(0, first, size) for first in firsts]]
    remote_grads.append(split(received(1, 0, rows)))
    weights = initial
    remote_weights = mixed(weights, "replica", 1)
    tracking = split(tracker[0])
    previous = split(last_grad[0])
    moment_one = split(first_moment[0])
    moment_two = split(second_moment[0])
    order = ()
    for step in range(step_count):
        last = step + 1 == step_count
        for part in parts:
            own = gradient_rows(step, place, firsts[part], size)
            mean_grad = (own + remote_grads[step][part]) * inverse_count
            known = after(remote_tracking[part], *order)
            tracking[part] = 0.5 * (tracking[part] + known) + mean_grad - previous[part]
            previous[part] = mean_grad
            tracking[part] = lax.optimization_barrier(tracking[part])
            order = (tracking[part],)
        if not last:
            for part in parts:
                remote_tracking[part] = shifted(tracking[part], "replica", 2 ** ((step + 1) % span_bits))
        update = []
        settled = [after(tracking[part], tracking[-1]) for part in parts]
        for part in parts:
            moment_one[part] = BETA_ONE * moment_one[part] + (1.0 - BETA_ONE) * settled[part]
            moment_two[part] = BETA_TWO * moment_two[part] + (1.0 - BETA_TWO) * settled[part] * settled[part]
            update.append(LEARNING_RATE * moment_one[part] / (jnp.sqrt(moment_two[part]) + EPSILON))
        update = jnp.concatenate(update, 0)
        if step > 0:
            weights = after(weights, tracking[-1])
            remote_weights = mixed(weights, "replica", 2 ** (step % span_bits))
        if step + 2 < step_count:
            remote_grads.append(split(received(step + 2, 0, rows, tracking[-1])))
        if last:
            settled_weights = 0.5 * weights - update - initial
            settled_weights = lax.optimization_barrier(settled_weights)
            change = (settled_weights + 0.5 * remote_weights) / LEARNING_RATE
        else:
            update = lax.optimization_barrier(update)
            order = (update,)
            weights = 0.5 * (weights + remote_weights) - update
            if step == 0:
                weights = lax.optimization_barrier(weights)
                order = (weights,)
            else:
                remote_tracking[-1], weights = lax.optimization_barrier((remote_tracking[-1], weights))
    return (change[None], jnp.concatenate(moment_one, 0)[None], jnp.concatenate(moment_two, 0)[None])


def solution(mesh):
    in_specs = (
        P("replica", "fsdp", None),
        P("replica", "fsdp", None),
        P("replica", "fsdp", None),
        P("replica", "fsdp", None),
        P("replica", "fsdp", None),
        P(None, "replica", "fsdp", None, None),
    )
    out_specs = (P("replica", "fsdp", None), P("replica", "fsdp", None), P("replica", "fsdp", None))
    return jax.shard_map(
        per_device, mesh=mesh, in_specs=in_specs, out_specs=out_specs, check_vma=False
    )
```

```python
import jax
import jax.numpy as jnp
from jax import lax
from jax.sharding import PartitionSpec as P

LEARNING_RATE = 0.001
BETA_ONE = 0.9
BETA_TWO = 0.999
EPSILON = 1e-08
PART = 8


def shifted(value, axis, steps):
    count = lax.axis_size(axis)
    pairs = [(source, (source + steps) % count) for source in range(count)]
    return lax.ppermute(value, axis, pairs)


def swapped(value, axis, distance):
    count = lax.axis_size(axis)
    pairs = [(source, source ^ distance) for source in range(count)]
    return lax.ppermute(value, axis, pairs)


def after(value, *others):
    return lax.optimization_barrier((value, *others))[0]


def per_device(params, tracker, last_grad, first_moment, second_moment, local_grads):
    initial = params[0]
    rows, columns = initial.shape
    replicas = lax.axis_size("replica")
    span_bits = replicas.bit_length() - 1
    fsdp = lax.axis_size("fsdp")
    place = lax.axis_index("fsdp")
    inverse_count = 1.0 / fsdp
    step_count = local_grads.shape[0]
    whole_span = step_count == span_bits and replicas == 2**span_bits
    mixed = swapped if whole_span else shifted
    size = PART if rows % PART == 0 else rows
    firsts = range(0, rows, size)
    parts = range(len(firsts))
    split = lambda whole: [whole[first : first + size] for first in firsts]

    def gradient_rows(step, keeper, first, count, *needed):
        source = after(local_grads, *needed) if needed else local_grads
        begin = (step, 0, 0, keeper * rows + first, 0)
        return lax.dynamic_slice(source, begin, (1, 1, 1, count, columns))[0, 0, 0].astype(jnp.float32)

    def received(step, first, count, *needed):
        pieces = []
        for distance in range(1, fsdp):
            outgoing = lax.optimization_barrier(gradient_rows(step, (place + distance) % fsdp, first, count, *needed))
            pieces.append(shifted(outgoing, "fsdp", distance))
        return sum(pieces) if pieces else jnp.zeros((count, columns), jnp.float32)

    remote_tracking = split(shifted(tracker[0], "replica", 1))
    remote_grads = [[received(0, first, size) for first in firsts]]
    remote_grads.append(split(received(1, 0, rows)))
    weights = initial
    remote_weights = mixed(weights, "replica", 1)
    tracking = split(tracker[0])
    previous = split(last_grad[0])
    moment_one = split(first_moment[0])
    moment_two = split(second_moment[0])
    begun = lax.optimization_barrier([0.5 * (tracking[part] + remote_tracking[part]) - previous[part] for part in parts])
    remote_grads[0] = [after(grads, *begun) for grads in remote_grads[0]]

    def moments(known):
        update = []
        for part in parts:
            moment_one[part] = BETA_ONE * moment_one[part] + (1.0 - BETA_ONE) * known[part]
            moment_two[part] = BETA_TWO * moment_two[part] + (1.0 - BETA_TWO) * known[part] * known[part]
            update.append(LEARNING_RATE * moment_one[part] / (jnp.sqrt(moment_two[part]) + EPSILON))
        return jnp.concatenate(update, 0)

    order = ()
    for step in range(step_count):
        last = step + 1 == step_count
        if last:
            weights = 0.5 * (weights + remote_weights) - moments(tracking)
            weights = lax.optimization_barrier(weights)
            remote_weights = mixed(weights, "replica", 2 ** (step % span_bits))
            order = (weights,)
        for part in parts:
            if 0 < step and part == len(parts) - 1 and not last:
                update = lax.optimization_barrier(moments([after(before[done], *order) for done in parts]))
                weights = 0.5 * (weights + after(remote_weights, *order)) - update
                weights = lax.optimization_barrier(weights)
                order = (weights, *order)
                if step + 2 == step_count:
                    remote_weights = mixed(weights, "replica", 2 ** (step % span_bits))
            own = gradient_rows(step, place, firsts[part], size)
            mean_grad = (own + remote_grads[step][part]) * inverse_count
            if step == 0:
                now = after(begun[part], *order) + mean_grad
            else:
                known = after(remote_tracking[part], *order)
                now = 0.5 * (tracking[part] + known) + mean_grad - previous[part]
            previous[part] = mean_grad
            if part == 0:
                before = list(tracking)
            tracking[part] = lax.optimization_barrier(now)
            order = (tracking[part],)
            if not last:
                remote_tracking[part] = shifted(tracking[part], "replica", 2 ** ((step + 1) % span_bits))
            if part == 0 and step + 2 < step_count:
                remote_grads.append(split(received(step + 2, 0, rows, tracking[part])))
        if 0 < step and not last and not (step + 2 == step_count):
            weights = after(weights, tracking[-1])
            remote_weights = mixed(weights, "replica", 2 ** (step % span_bits))
    update = moments(tracking)
    settled_weights = lax.optimization_barrier(0.5 * weights - update - initial)
    change = (settled_weights + 0.5 * remote_weights) / LEARNING_RATE
    return (change[None], jnp.concatenate(moment_one, 0)[None], jnp.concatenate(moment_two, 0)[None])


def solution(mesh):
    in_specs = (
        P("replica", "fsdp", None),
        P("replica", "fsdp", None),
        P("replica", "fsdp", None),
        P("replica", "fsdp", None),
        P("replica", "fsdp", None),
        P(None, "replica", "fsdp", None, None),
    )
    out_specs = (P("replica", "fsdp", None), P("replica", "fsdp", None), P("replica", "fsdp", None))
    return jax.shard_map(
        per_device, mesh=mesh, in_specs=in_specs, out_specs=out_specs, check_vma=False
    )
```

```python
import jax
import jax.numpy as jnp
from jax import lax
from jax.sharding import PartitionSpec as P

LEARNING_RATE = 0.001
BETA_ONE = 0.9
BETA_TWO = 0.999
EPSILON = 1e-08
PART = 8


def shifted(value, axis, steps):
    count = lax.axis_size(axis)
    pairs = [(source, (source + steps) % count) for source in range(count)]
    return lax.ppermute(value, axis, pairs)


def swapped(value, axis, distance):
    count = lax.axis_size(axis)
    pairs = [(source, source ^ distance) for source in range(count)]
    return lax.ppermute(value, axis, pairs)


def after(value, *others):
    return lax.optimization_barrier((value, *others))[0]


def per_device(params, tracker, last_grad, first_moment, second_moment, local_grads):
    initial = params[0]
    rows, columns = initial.shape
    replicas = lax.axis_size("replica")
    span_bits = replicas.bit_length() - 1
    fsdp = lax.axis_size("fsdp")
    place = lax.axis_index("fsdp")
    inverse_count = 1.0 / fsdp
    step_count = local_grads.shape[0]
    whole_span = step_count == span_bits and replicas == 2**span_bits
    mixed = swapped if whole_span else shifted
    size = PART if rows % PART == 0 else rows
    firsts = range(0, rows, size)
    parts = range(len(firsts))
    split = lambda whole: [whole[first : first + size] for first in firsts]

    def gradient_rows(step, keeper, first, count, *needed):
        source = after(local_grads, *needed) if needed else local_grads
        begin = (step, 0, 0, keeper * rows + first, 0)
        return lax.dynamic_slice(source, begin, (1, 1, 1, count, columns))[0, 0, 0].astype(jnp.float32)

    def received(step, first, count, *needed):
        pieces = []
        for distance in range(1, fsdp):
            outgoing = lax.optimization_barrier(gradient_rows(step, (place + distance) % fsdp, first, count, *needed))
            pieces.append(shifted(outgoing, "fsdp", distance))
        return sum(pieces) if pieces else jnp.zeros((count, columns), jnp.float32)

    remote_tracking = split(shifted(tracker[0], "replica", 1))
    remote_grads = [[received(0, first, size) for first in firsts]]
    remote_grads.append(split(received(1, 0, rows)))
    weights = initial
    remote_weights = mixed(weights, "replica", 1)
    tracking = split(tracker[0])
    previous = split(last_grad[0])
    moment_one = split(first_moment[0])
    moment_two = split(second_moment[0])
    begun = lax.optimization_barrier([0.5 * (tracking[part] + remote_tracking[part]) - previous[part] for part in parts])
    remote_grads[0] = [after(grads, *begun) for grads in remote_grads[0]]

    def moment_part(part, known):
        moment_one[part] = BETA_ONE * moment_one[part] + (1.0 - BETA_ONE) * known
        moment_two[part] = BETA_TWO * moment_two[part] + (1.0 - BETA_TWO) * known * known
        return LEARNING_RATE * moment_one[part] / (jnp.sqrt(moment_two[part]) + EPSILON)

    def moments(known):
        return jnp.concatenate([moment_part(part, known[part]) for part in parts], 0)

    order = ()
    for step in range(step_count):
        last = step + 1 == step_count
        if last:
            for part in parts:
                now = 0.5 * (pieces[part] + after(remote_pieces[part], *order)) - moment_part(part, tracking[part])
                pieces[part] = lax.optimization_barrier(now)
                remote_pieces[part] = mixed(pieces[part], "replica", 2 ** (step % span_bits))
                order = (pieces[part],)
        for part in parts:
            if 0 < step and part == len(parts) - 1 and not last:
                update = lax.optimization_barrier(moments([after(before[done], *order) for done in parts]))
                weights = 0.5 * (weights + after(remote_weights, *order)) - update
                weights = lax.optimization_barrier(weights)
                order = (weights, *order)
                if step + 2 == step_count:
                    pieces = lax.optimization_barrier(split(weights))
                    remote_pieces = [mixed(piece, "replica", 2 ** (step % span_bits)) for piece in pieces]
            own = gradient_rows(step, place, firsts[part], size)
            mean_grad = (own + remote_grads[step][part]) * inverse_count
            if step == 0:
                now = after(begun[part], *order) + mean_grad
            else:
                known = after(remote_tracking[part], *order)
                now = 0.5 * (tracking[part] + known) + mean_grad - previous[part]
            previous[part] = mean_grad
            if part == 0:
                before = list(tracking)
            tracking[part] = lax.optimization_barrier(now)
            order = (tracking[part],)
            if not last:
                remote_tracking[part] = shifted(tracking[part], "replica", 2 ** ((step + 1) % span_bits))
            if part == 0 and step + 2 < step_count:
                remote_grads.append(split(received(step + 2, 0, rows, tracking[part])))
        if 0 < step and not last and not (step + 2 == step_count):
            weights = after(weights, tracking[-1])
            remote_weights = mixed(weights, "replica", 2 ** (step % span_bits))
    begin = split(initial)
    settled = lax.optimization_barrier([0.5 * pieces[part] - moment_part(part, tracking[part]) - begin[part] for part in parts])
    change = jnp.concatenate([(settled[part] + 0.5 * remote_pieces[part]) / LEARNING_RATE for part in parts], 0)
    return (change[None], jnp.concatenate(moment_one, 0)[None], jnp.concatenate(moment_two, 0)[None])


def solution(mesh):
    in_specs = (
        P("replica", "fsdp", None),
        P("replica", "fsdp", None),
        P("replica", "fsdp", None),
        P("replica", "fsdp", None),
        P("replica", "fsdp", None),
        P(None, "replica", "fsdp", None, None),
    )
    out_specs = (P("replica", "fsdp", None), P("replica", "fsdp", None), P("replica", "fsdp", None))
    return jax.shard_map(
        per_device, mesh=mesh, in_specs=in_specs, out_specs=out_specs, check_vma=False
    )
```

```python
import jax
import jax.numpy as jnp
from jax import lax
from jax.sharding import PartitionSpec as P

LEARNING_RATE = 0.001
BETA_ONE = 0.9
BETA_TWO = 0.999
EPSILON = 1e-08
PART = 8


def shifted(value, axis, steps):
    count = lax.axis_size(axis)
    pairs = [(source, (source + steps) % count) for source in range(count)]
    return lax.ppermute(value, axis, pairs)


def swapped(value, axis, distance):
    count = lax.axis_size(axis)
    pairs = [(source, source ^ distance) for source in range(count)]
    return lax.ppermute(value, axis, pairs)


def after(value, *others):
    return lax.optimization_barrier((value, *others))[0]


def per_device(params, tracker, last_grad, first_moment, second_moment, local_grads):
    initial = params[0]
    rows, columns = initial.shape
    replicas = lax.axis_size("replica")
    span_bits = replicas.bit_length() - 1
    fsdp = lax.axis_size("fsdp")
    place = lax.axis_index("fsdp")
    inverse_count = 1.0 / fsdp
    step_count = local_grads.shape[0]
    whole_span = step_count == span_bits and replicas == 2**span_bits
    mixed = swapped if whole_span else shifted
    size = PART if rows % PART == 0 else rows
    firsts = range(0, rows, size)
    parts = range(len(firsts))
    split = lambda whole: [whole[first : first + size] for first in firsts]

    def gradient_rows(step, keeper, first, count, *needed):
        source = after(local_grads, *needed) if needed else local_grads
        begin = (step, 0, 0, keeper * rows + first, 0)
        return lax.dynamic_slice(source, begin, (1, 1, 1, count, columns))[0, 0, 0].astype(jnp.float32)

    def packed(pieces, *needed):
        return lax.optimization_barrier([
            [gradient_rows(step, (place + distance) % fsdp, first, count, *needed) for step, first, count in pieces]
            for distance in range(1, fsdp)
        ])

    def sent(packs, chosen, *needed):
        totals = [jnp.zeros((1, 1), jnp.float32)] * len(chosen)
        for distance, values in enumerate(packs, 1):
            values = [values[number] for number in chosen]
            if needed:
                values = lax.optimization_barrier((values, needed))[0]
            pieces = [shifted(value, "fsdp", distance) for value in values]
            totals = pieces if distance == 1 else [total + piece for total, piece in zip(totals, pieces)]
        return totals

    def moment_part(part, known):
        moment_one[part] = BETA_ONE * moment_one[part] + (1.0 - BETA_ONE) * known
        moment_two[part] = BETA_TWO * moment_two[part] + (1.0 - BETA_TWO) * known * known
        return LEARNING_RATE * moment_one[part] / (jnp.sqrt(moment_two[part]) + EPSILON)

    def distance_of(step):
        return 2 ** (step % span_bits)

    def swap_out(pieces, step):
        return [mixed(piece, "replica", distance_of(step)) for piece in pieces]

    remote_tracking = split(shifted(tracker[0], "replica", 1))
    tracking = split(tracker[0])
    previous = split(last_grad[0])
    moment_one = split(first_moment[0])
    moment_two = split(second_moment[0])
    begin = split(initial)
    other = parts[-1]
    remote_grads = [[None for _ in parts] for _ in range(step_count)]
    pack = packed([(0, first, size) for first in firsts[:1]])
    later = packed([(0, first, size) for first in firsts[1:]] + [(1, first, size) for first in firsts], *sum(pack, []))
    shift = other
    remote_grads[0] = sent(pack, [0]) + sent(later, range(shift))
    remote_grads[1] = sent(later, range(shift, shift + len(firsts)))
    weights = [initial]
    remote_weights = swap_out(weights, 0)
    ready = after(last_grad[0], *sum(later, []))
    whole = lax.optimization_barrier(0.5 * tracker[0] - ready)
    base = split(whole)
    begun = [base[part] + 0.5 * remote_tracking[part] for part in parts]
    order = ()
    for step in range(step_count):
        last = step + 1 == step_count
        if last:
            for part in parts:
                now = 0.5 * (pieces[part] + after(remote_pieces[part], *order)) - moment_part(part, tracking[part])
                pieces[part] = lax.optimization_barrier(now)
                remote_pieces[part] = mixed(pieces[part], "replica", distance_of(step))
                order = (pieces[part],)
        for part in parts:
            if 0 < step and part == other and not last:
                update = [moment_part(done, after(before[done], *order)) for done in parts]
                update = lax.optimization_barrier(update)
                if step == 1:
                    whole = lax.optimization_barrier(weights[0] - jnp.concatenate(update, 0))
                    weights = lax.optimization_barrier(split(whole)) if False else [whole]
                else:
                    pairs = zip(weights, remote_weights)
                    mean = [0.5 * (weight + after(remote, *order)) for weight, remote in pairs]
                    whole = mean[0] if len(mean) == 1 else jnp.concatenate(mean, 0)
                    if len(mean) == 1:
                        whole = lax.optimization_barrier(whole - jnp.concatenate(update, 0))
                        weights = [whole]
                    else:
                        weights = lax.optimization_barrier([value - taken for value, taken in zip(mean, update)])
                    order = (*weights, *order)
                if step + 2 == step_count:
                    pieces = weights if len(weights) > 1 else lax.optimization_barrier(split(weights[0]))
                    remote_pieces = swap_out(pieces, step)
                elif step == 1:
                    remote_weights = swap_out(weights, step)
                    order = (*weights, *order)
            own = gradient_rows(step, place, firsts[part], size)
            mean_grad = (own + remote_grads[step][part]) * inverse_count
            if step == 0:
                now = after(begun[part], *order) + mean_grad
            else:
                known = after(remote_tracking[part], *order)
                now = 0.5 * (tracking[part] + known) + mean_grad - previous[part]
            previous[part] = mean_grad
            if part == 0:
                before = list(tracking)
            tracking[part] = lax.optimization_barrier(now)
            order = (tracking[part],)
            if not last:
                remote_tracking[part] = shifted(tracking[part], "replica", distance_of(step + 1))
            if step == 0 and part == other:
                weights = lax.optimization_barrier([0.5 * (weights[0] + after(remote_weights[0], *order))])
                order = (*weights, *order)
            if (step, part) == (0, 0) and 2 < step_count:
                remote_grads[2] = split(sent(packed([(2, 0, rows)], tracking[part]), [0])[0])
            if part == 0:
                for number in range(3, step_count):
                    if step == number - 3 + 1:
                        remote_grads[number] = split(sent(packed([(number, 0, rows)], tracking[part]), [0])[0])
        if step == 1 and not last:
            pass
    settled = [0.5 * pieces[part] - moment_part(part, tracking[part]) - begin[part] for part in parts]
    settled = lax.optimization_barrier(settled)
    change = jnp.concatenate([(settled[part] + 0.5 * remote_pieces[part]) / LEARNING_RATE for part in parts], 0)
    return (change[None], jnp.concatenate(moment_one, 0)[None], jnp.concatenate(moment_two, 0)[None])


def solution(mesh):
    in_specs = (
        P("replica", "fsdp", None),
        P("replica", "fsdp", None),
        P("replica", "fsdp", None),
        P("replica", "fsdp", None),
        P("replica", "fsdp", None),
        P(None, "replica", "fsdp", None, None),
    )
    out_specs = (P("replica", "fsdp", None), P("replica", "fsdp", None), P("replica", "fsdp", None))
    return jax.shard_map(
        per_device, mesh=mesh, in_specs=in_specs, out_specs=out_specs, check_vma=False
    )
```

```python
import jax
import jax.numpy as jnp
from jax import lax
from jax.sharding import PartitionSpec as P

LEARNING_RATE = 0.001
BETA_ONE = 0.9
BETA_TWO = 0.999
EPSILON = 1e-08
PART = 8


def shifted(value, axis, steps):
    count = lax.axis_size(axis)
    pairs = [(source, (source + steps) % count) for source in range(count)]
    return lax.ppermute(value, axis, pairs)


def swapped(value, axis, distance):
    count = lax.axis_size(axis)
    pairs = [(source, source ^ distance) for source in range(count)]
    return lax.ppermute(value, axis, pairs)


def after(value, *others):
    return lax.optimization_barrier((value, *others))[0]


def per_device(params, tracker, last_grad, first_moment, second_moment, local_grads):
    initial = params[0]
    rows, columns = initial.shape
    replicas = lax.axis_size("replica")
    span_bits = replicas.bit_length() - 1
    fsdp = lax.axis_size("fsdp")
    place = lax.axis_index("fsdp")
    inverse_count = 1.0 / fsdp
    step_count = local_grads.shape[0]
    whole_span = step_count == span_bits and replicas == 2**span_bits
    mixed = swapped if whole_span else shifted
    size = PART if rows % PART == 0 else rows
    firsts = range(0, rows, size)
    parts = range(len(firsts))
    split = lambda whole: [whole[first : first + size] for first in firsts]

    def gradient_rows(step, keeper, first, count, *needed):
        source = after(local_grads, *needed) if needed else local_grads
        begin = (step, 0, 0, keeper * rows + first, 0)
        return lax.dynamic_slice(source, begin, (1, 1, 1, count, columns))[0, 0, 0].astype(jnp.float32)

    def packed(pieces, *needed):
        return lax.optimization_barrier([
            [gradient_rows(step, (place + distance) % fsdp, first, count, *needed) for step, first, count in pieces]
            for distance in range(1, fsdp)
        ])

    def sent(packs, chosen, *needed):
        totals = [jnp.zeros((1, 1), jnp.float32)] * len(chosen)
        for distance, values in enumerate(packs, 1):
            values = [values[number] for number in chosen]
            if needed:
                values = lax.optimization_barrier((values, needed))[0]
            pieces = [shifted(value, "fsdp", distance) for value in values]
            totals = pieces if distance == 1 else [total + piece for total, piece in zip(totals, pieces)]
        return totals

    def moment_part(part, known):
        moment_one[part] = BETA_ONE * moment_one[part] + (1.0 - BETA_ONE) * known
        moment_two[part] = BETA_TWO * moment_two[part] + (1.0 - BETA_TWO) * known * known
        return LEARNING_RATE * moment_one[part] / (jnp.sqrt(moment_two[part]) + EPSILON)

    def distance_of(step):
        return 2 ** (step % span_bits)

    def swap_out(pieces, step):
        return [mixed(piece, "replica", distance_of(step)) for piece in pieces]

    remote_tracking = split(shifted(tracker[0], "replica", 1))
    tracking = split(tracker[0])
    previous = split(last_grad[0])
    moment_one = split(first_moment[0])
    moment_two = split(second_moment[0])
    begin = split(initial)
    other = parts[-1]
    remote_grads = [[None for _ in parts] for _ in range(step_count)]
    pack = packed([(0, first, size) for first in firsts[:1]])
    later = packed([(0, first, size) for first in firsts[1:]] + [(1, first, size) for first in firsts], *sum(pack, []))
    shift = other
    remote_grads[0] = sent(pack, [0]) + sent(later, range(shift))
    remote_grads[1] = sent(later, [shift])
    weights = [initial]
    remote_weights = swap_out(weights, 0)
    ready = after(last_grad[0], *sum(later, []))
    whole = lax.optimization_barrier(0.5 * tracker[0] - ready)
    base = split(whole)
    begun = [base[part] + 0.5 * remote_tracking[part] for part in parts]
    order = ()
    for step in range(step_count):
        last = step + 1 == step_count
        if last:
            for part in parts:
                now = 0.5 * (pieces[part] + after(remote_pieces[part], *order)) - moment_part(part, tracking[part])
                pieces[part] = lax.optimization_barrier(now)
                remote_pieces[part] = mixed(pieces[part], "replica", distance_of(step))
                order = (pieces[part],)
        for part in parts:
            if 0 < step and part == other and not last:
                update = [moment_part(done, after(before[done], *order)) for done in parts]
                update = lax.optimization_barrier(update)
                if step == 1:
                    whole = lax.optimization_barrier(weights[0] - jnp.concatenate(update, 0))
                    weights = lax.optimization_barrier(split(whole)) if False else [whole]
                else:
                    pairs = zip(weights, remote_weights)
                    mean = [0.5 * (weight + after(remote, *order)) for weight, remote in pairs]
                    whole = mean[0] if len(mean) == 1 else jnp.concatenate(mean, 0)
                    if len(mean) == 1:
                        whole = lax.optimization_barrier(whole - jnp.concatenate(update, 0))
                        weights = [whole]
                    else:
                        weights = lax.optimization_barrier([value - taken for value, taken in zip(mean, update)])
                    order = (*weights, *order)
                if step + 2 == step_count:
                    pieces = weights if len(weights) > 1 else lax.optimization_barrier(split(weights[0]))
                    remote_pieces = swap_out(pieces, step)
                elif step == 1:
                    remote_weights = swap_out(weights, step)
                    order = (*weights, *order)
            own = gradient_rows(step, place, firsts[part], size)
            mean_grad = (own + remote_grads[step][part]) * inverse_count
            if step == 0:
                now = after(begun[part], *order) + mean_grad
            else:
                known = after(remote_tracking[part], *order)
                now = 0.5 * (tracking[part] + known) + mean_grad - previous[part]
            previous[part] = mean_grad
            if part == 0:
                before = list(tracking)
            tracking[part] = lax.optimization_barrier(now)
            order = (tracking[part],)
            if not last:
                remote_tracking[part] = shifted(tracking[part], "replica", distance_of(step + 1))
            if step == 0 and part == 0:
                weights = lax.optimization_barrier([0.5 * (weights[0] + after(remote_weights[0], *order))])
                order = (*weights, *order)
            if step == 0 and part == other:
                remote_grads[1] += sent(later, range(shift + 1, shift + len(firsts)), tracking[part])
            if (step, part) == (0, other) and 2 < step_count:
                remote_grads[2] = split(sent(packed([(2, 0, rows)], tracking[part]), [0])[0])
            if part == 0:
                for number in range(3, step_count):
                    if step == number - 3 + 2:
                        remote_grads[number] = split(sent(packed([(number, 0, rows)], tracking[part]), [0])[0])
        if step == 1 and not last:
            pass
    settled = [0.5 * pieces[part] - moment_part(part, tracking[part]) - begin[part] for part in parts]
    settled = lax.optimization_barrier(settled)
    change = jnp.concatenate([(settled[part] + 0.5 * remote_pieces[part]) / LEARNING_RATE for part in parts], 0)
    return (change[None], jnp.concatenate(moment_one, 0)[None], jnp.concatenate(moment_two, 0)[None])


def solution(mesh):
    in_specs = (
        P("replica", "fsdp", None),
        P("replica", "fsdp", None),
        P("replica", "fsdp", None),
        P("replica", "fsdp", None),
        P("replica", "fsdp", None),
        P(None, "replica", "fsdp", None, None),
    )
    out_specs = (P("replica", "fsdp", None), P("replica", "fsdp", None), P("replica", "fsdp", None))
    return jax.shard_map(
        per_device, mesh=mesh, in_specs=in_specs, out_specs=out_specs, check_vma=False
    )
```

```python
import jax
import jax.numpy as jnp
from jax import lax
from jax.sharding import PartitionSpec as P

LEARNING_RATE = 0.001
BETA_ONE = 0.9
BETA_TWO = 0.999
EPSILON = 1e-08
PART = 8


def shifted(value, axis, steps):
    count = lax.axis_size(axis)
    pairs = [(source, (source + steps) % count) for source in range(count)]
    return lax.ppermute(value, axis, pairs)


def swapped(value, axis, distance):
    count = lax.axis_size(axis)
    pairs = [(source, source ^ distance) for source in range(count)]
    return lax.ppermute(value, axis, pairs)


def after(value, *others):
    return lax.optimization_barrier((value, *others))[0]


def per_device(params, tracker, last_grad, first_moment, second_moment, local_grads):
    initial = params[0]
    rows, columns = initial.shape
    replicas = lax.axis_size("replica")
    span_bits = replicas.bit_length() - 1
    fsdp = lax.axis_size("fsdp")
    place = lax.axis_index("fsdp")
    inverse_count = 1.0 / fsdp
    step_count = local_grads.shape[0]
    whole_span = step_count == span_bits and replicas == 2**span_bits
    mixed = swapped if whole_span else shifted
    size = PART if rows % PART == 0 else rows
    firsts = range(0, rows, size)
    parts = range(len(firsts))
    split = lambda whole: [whole[first : first + size] for first in firsts]

    def gradient_rows(step, keeper, first, count, *needed):
        source = after(local_grads, *needed) if needed else local_grads
        begin = (step, 0, 0, keeper * rows + first, 0)
        return lax.dynamic_slice(source, begin, (1, 1, 1, count, columns))[0, 0, 0].astype(jnp.float32)

    def packed(pieces, *needed):
        return lax.optimization_barrier([
            [gradient_rows(step, (place + distance) % fsdp, first, count, *needed) for step, first, count in pieces]
            for distance in range(1, fsdp)
        ])

    def sent(packs, chosen, *needed):
        totals = [jnp.zeros((1, 1), jnp.float32)] * len(chosen)
        for distance, values in enumerate(packs, 1):
            values = [values[number] for number in chosen]
            if needed:
                values = lax.optimization_barrier((values, needed))[0]
            pieces = [shifted(value, "fsdp", distance) for value in values]
            totals = pieces if distance == 1 else [total + piece for total, piece in zip(totals, pieces)]
        return totals

    def moment_part(part, known):
        moment_one[part] = BETA_ONE * moment_one[part] + (1.0 - BETA_ONE) * known
        moment_two[part] = BETA_TWO * moment_two[part] + (1.0 - BETA_TWO) * known * known
        return LEARNING_RATE * moment_one[part] / (jnp.sqrt(moment_two[part]) + EPSILON)

    def distance_of(step):
        return 2 ** (step % span_bits)

    def swap_out(pieces, step):
        return [mixed(piece, "replica", distance_of(step)) for piece in pieces]

    remote_tracking = split(shifted(tracker[0], "replica", 1))
    tracking = split(tracker[0])
    previous = split(last_grad[0])
    moment_one = split(first_moment[0])
    moment_two = split(second_moment[0])
    begin = split(initial)
    other = parts[-1]
    remote_grads = [[None for _ in parts] for _ in range(step_count)]
    pack = packed([(0, first, size) for first in firsts[:1]])
    later = packed([(0, first, size) for first in firsts[1:]] + [(1, first, size) for first in firsts], *sum(pack, []))
    shift = other
    remote_grads[0] = sent(pack, [0]) + sent(later, range(shift))
    remote_grads[1] = sent(later, [shift])
    weights = [initial]
    remote_weights = swap_out(weights, 0)
    ready = after(last_grad[0], *sum(later, []))
    whole = lax.optimization_barrier(0.5 * tracker[0] - ready)
    base = split(whole)
    begun = [base[part] + 0.5 * remote_tracking[part] for part in parts]
    order = ()
    for step in range(step_count):
        last = step + 1 == step_count
        if last:
            for part in parts:
                taken = lax.optimization_barrier(moment_part(part, tracking[part]))
                now = 0.5 * (pieces[part] + after(remote_pieces[part], *order)) - taken
                pieces[part] = lax.optimization_barrier(now)
                remote_pieces[part] = mixed(pieces[part], "replica", distance_of(step))
                order = (pieces[part], *order)
        for part in parts:
            if 0 < step and part == other and not last:
                update = [moment_part(done, after(before[done], *order)) for done in parts]
                update = lax.optimization_barrier(update)
                if step == 1:
                    whole = lax.optimization_barrier(weights[0] - jnp.concatenate(update, 0))
                    weights = lax.optimization_barrier(split(whole)) if False else [whole]
                else:
                    pairs = zip(weights, remote_weights)
                    mean = [0.5 * (weight + after(remote, *order)) for weight, remote in pairs]
                    whole = mean[0] if len(mean) == 1 else jnp.concatenate(mean, 0)
                    if len(mean) == 1:
                        whole = lax.optimization_barrier(whole - jnp.concatenate(update, 0))
                        weights = [whole]
                    else:
                        weights = lax.optimization_barrier([value - taken for value, taken in zip(mean, update)])
                    order = (*weights, *order)
                if step + 2 == step_count:
                    pieces = weights if len(weights) > 1 else lax.optimization_barrier(split(weights[0]))
                    remote_pieces = swap_out(pieces, step)
                elif step == 1:
                    remote_weights = swap_out(weights, step)
                    order = (*weights, *order)
            own = gradient_rows(step, place, firsts[part], size)
            mean_grad = (own + remote_grads[step][part]) * inverse_count
            if step == 0:
                now = after(begun[part], *order) + mean_grad
            else:
                known = after(remote_tracking[part], *order)
                now = 0.5 * (tracking[part] + known) + mean_grad - previous[part]
            previous[part] = mean_grad
            if part == 0:
                before = list(tracking)
            tracking[part] = lax.optimization_barrier(now)
            order = (tracking[part],)
            if not last:
                remote_tracking[part] = shifted(tracking[part], "replica", distance_of(step + 1))
            if step == 0 and part == 0:
                weights = lax.optimization_barrier([0.5 * (weights[0] + after(remote_weights[0], *order))])
                order = (*weights, *order)
            if step == 0 and part == other:
                remote_grads[1] += sent(later, range(shift + 1, shift + len(firsts)), tracking[part])
            if (step, part) == (0, other) and 2 < step_count:
                remote_grads[2] = split(sent(packed([(2, 0, rows)], tracking[part]), [0])[0])
            if part == 0:
                for number in range(3, step_count):
                    if step == number - 3 + 2:
                        remote_grads[number] = split(sent(packed([(number, 0, rows)], tracking[part]), [0])[0])
        if step == 1 and not last:
            pass
    settled = [0.5 * pieces[part] - moment_part(part, tracking[part]) - begin[part] for part in parts]
    settled = lax.optimization_barrier(settled)
    change = jnp.concatenate([(settled[part] + 0.5 * remote_pieces[part]) / LEARNING_RATE for part in parts], 0)
    return (change[None], jnp.concatenate(moment_one, 0)[None], jnp.concatenate(moment_two, 0)[None])


def solution(mesh):
    in_specs = (
        P("replica", "fsdp", None),
        P("replica", "fsdp", None),
        P("replica", "fsdp", None),
        P("replica", "fsdp", None),
        P("replica", "fsdp", None),
        P(None, "replica", "fsdp", None, None),
    )
    out_specs = (P("replica", "fsdp", None), P("replica", "fsdp", None), P("replica", "fsdp", None))
    return jax.shard_map(
        per_device, mesh=mesh, in_specs=in_specs, out_specs=out_specs, check_vma=False
    )
```

```python
import jax
import jax.numpy as jnp
from jax import lax
from jax.sharding import PartitionSpec as P

LEARNING_RATE = 0.001
BETA_ONE = 0.9
BETA_TWO = 0.999
EPSILON = 1e-08
PART = 8


def shifted(value, axis, steps):
    count = lax.axis_size(axis)
    pairs = [(source, (source + steps) % count) for source in range(count)]
    return lax.ppermute(value, axis, pairs)


def swapped(value, axis, distance):
    count = lax.axis_size(axis)
    pairs = [(source, source ^ distance) for source in range(count)]
    return lax.ppermute(value, axis, pairs)


def after(value, *others):
    return lax.optimization_barrier((value, *others))[0]


def per_device(params, tracker, last_grad, first_moment, second_moment, local_grads):
    initial = params[0]
    rows, columns = initial.shape
    replicas = lax.axis_size("replica")
    span_bits = replicas.bit_length() - 1
    fsdp = lax.axis_size("fsdp")
    place = lax.axis_index("fsdp")
    inverse_count = 1.0 / fsdp
    step_count = local_grads.shape[0]
    whole_span = step_count == span_bits and replicas == 2**span_bits
    mixed = swapped if whole_span else shifted
    size = PART if rows % PART == 0 else rows
    firsts = range(0, rows, size)
    parts = range(len(firsts))
    split = lambda whole: [whole[first : first + size] for first in firsts]

    def gradient_rows(step, keeper, first, count, *needed):
        source = after(local_grads, *needed) if needed else local_grads
        begin = (step, 0, 0, keeper * rows + first, 0)
        return lax.dynamic_slice(source, begin, (1, 1, 1, count, columns))[0, 0, 0].astype(jnp.float32)

    def packed(pieces, *needed):
        return lax.optimization_barrier([
            [gradient_rows(step, (place + distance) % fsdp, first, count, *needed) for step, first, count in pieces]
            for distance in range(1, fsdp)
        ])

    def sent(packs, chosen, *needed):
        totals = [jnp.zeros((1, 1), jnp.float32)] * len(chosen)
        for distance, values in enumerate(packs, 1):
            values = [values[number] for number in chosen]
            if needed:
                values = lax.optimization_barrier((values, needed))[0]
            pieces = [shifted(value, "fsdp", distance) for value in values]
            totals = pieces if distance == 1 else [total + piece for total, piece in zip(totals, pieces)]
        return totals

    def moment_part(part, known):
        moment_one[part] = BETA_ONE * moment_one[part] + (1.0 - BETA_ONE) * known
        moment_two[part] = BETA_TWO * moment_two[part] + (1.0 - BETA_TWO) * known * known
        return LEARNING_RATE * moment_one[part] / (jnp.sqrt(moment_two[part]) + EPSILON)

    def distance_of(step):
        return 2 ** (step % span_bits)

    def swap_out(pieces, step):
        return [mixed(piece, "replica", distance_of(step)) for piece in pieces]

    remote_tracking = split(shifted(tracker[0], "replica", 1))
    tracking = split(tracker[0])
    previous = split(last_grad[0])
    moment_one = split(first_moment[0])
    moment_two = split(second_moment[0])
    begin = split(initial)
    other = parts[-1]
    remote_grads = [[None for _ in parts] for _ in range(step_count)]
    pack = packed([(0, first, size) for first in firsts[:1]])
    later = packed([(0, first, size) for first in firsts[1:]] + [(1, first, size) for first in firsts], *sum(pack, []))
    shift = other
    remote_grads[0] = sent(pack, [0]) + sent(later, range(shift))
    remote_grads[1] = sent(later, [shift])
    weights = [initial]
    remote_weights = swap_out(weights, 0)
    ready = after(last_grad[0], *sum(later, []))
    whole = lax.optimization_barrier(0.5 * tracker[0] - ready)
    base = split(whole)
    begun = [base[part] + 0.5 * remote_tracking[part] for part in parts]
    order = ()
    for step in range(step_count):
        last = step + 1 == step_count
        if last:
            for part in parts:
                now = 0.5 * (pieces[part] + after(remote_pieces[part], *order)) - moment_part(part, tracking[part])
                pieces[part] = lax.optimization_barrier(now)
                remote_pieces[part] = mixed(pieces[part], "replica", distance_of(step))
                order = (pieces[part],)
        for part in parts:
            if 0 < step and part == other and not last:
                update = [moment_part(done, after(before[done], *order)) for done in parts]
                update = lax.optimization_barrier(update)
                if step == 1:
                    whole = lax.optimization_barrier(weights[0] - jnp.concatenate(update, 0))
                    weights = lax.optimization_barrier(split(whole)) if False else [whole]
                else:
                    pairs = zip(weights, remote_weights)
                    mean = [0.5 * (weight + after(remote, *order)) for weight, remote in pairs]
                    whole = mean[0] if len(mean) == 1 else jnp.concatenate(mean, 0)
                    if len(mean) == 1:
                        whole = lax.optimization_barrier(whole - jnp.concatenate(update, 0))
                        weights = [whole]
                    else:
                        weights = lax.optimization_barrier([value - taken for value, taken in zip(mean, update)])
                    order = (*weights, *order)
                if step + 2 == step_count:
                    pieces = weights if len(weights) > 1 else lax.optimization_barrier(split(weights[0]))
                    remote_pieces = swap_out(pieces, step)
                elif step == 1:
                    remote_weights = swap_out(weights, step)
                    order = (*weights, *order)
            own = gradient_rows(step, place, firsts[part], size)
            mean_grad = (own + remote_grads[step][part]) * inverse_count
            if step == 0:
                now = after(begun[part], *order) + mean_grad
            else:
                known = after(remote_tracking[part], *order)
                now = 0.5 * (tracking[part] + known) + mean_grad - previous[part]
            previous[part] = mean_grad
            if part == 0:
                before = list(tracking)
            tracking[part] = lax.optimization_barrier(now)
            order = (tracking[part],)
            if not last:
                remote_tracking[part] = shifted(tracking[part], "replica", distance_of(step + 1))
            if step == 0 and part == 0:
                weights = lax.optimization_barrier([0.5 * (weights[0] + after(remote_weights[0], *order))])
                order = (*weights, *order)
            if step == 0 and part == other:
                remote_grads[1] += sent(later, range(shift + 1, shift + len(firsts)), tracking[part])
            if (step, part) == (0, 0) and 2 < step_count:
                remote_grads[2] = split(sent(packed([(2, 0, rows)], tracking[part]), [0])[0])
            if part == 0:
                for number in range(3, step_count):
                    if step == number - 3 + 2:
                        remote_grads[number] = split(sent(packed([(number, 0, rows)], tracking[part]), [0])[0])
        if step == 1 and not last:
            pass
    settled = [0.5 * pieces[part] - moment_part(part, tracking[part]) - begin[part] for part in parts]
    settled = lax.optimization_barrier(settled)
    change = jnp.concatenate([(settled[part] + 0.5 * remote_pieces[part]) / LEARNING_RATE for part in parts], 0)
    return (change[None], jnp.concatenate(moment_one, 0)[None], jnp.concatenate(moment_two, 0)[None])


def solution(mesh):
    in_specs = (
        P("replica", "fsdp", None),
        P("replica", "fsdp", None),
        P("replica", "fsdp", None),
        P("replica", "fsdp", None),
        P("replica", "fsdp", None),
        P(None, "replica", "fsdp", None, None),
    )
    out_specs = (P("replica", "fsdp", None), P("replica", "fsdp", None), P("replica", "fsdp", None))
    return jax.shard_map(
        per_device, mesh=mesh, in_specs=in_specs, out_specs=out_specs, check_vma=False
    )
```
